32 devices in a mesh: pair: 2 (over core), box: 4 (over y, x), tile: 4 (over z).
Axes of the slice: x: 2, y: 2, z: 4, core: 2. Of those that a mesh axis runs over, the one named last changes fastest.
Arguments:
- child_maps: bfloat16 [2, 16, 2304, 2304], P('pair', ('box', 'tile')), parts along dimension 1, as said below
- face_order: int32 [4, 2, 6], P('box'), parts along dimension 0, may hold values from 0 to 5, each once within a row
Outputs:
- parent_update: bfloat16 [2, 16, 1920, 1536], P('pair', ('box', 'tile')), parts along dimension 1
The draws below stay inside these ranges and needn't reach their ends.
There are 4 independent parts, one for each index of `box`. The reference program is written for one: setup_inputs(seed, part) draws one part's arguments, and reference() takes and returns one part's arrays. A program takes and returns all parts, laid end to end along the dimension named above; each array names one. Nothing has to cross between parts.
Inputs may be any that keep to these rules, and one draw needn't show every extreme that they name: Each row of face_order lists every face once: entry 0 is the child's shared face, entries 1 to 5 its exterior faces in parent order. `child_maps`: child maps are dense with independent entries.
All inputs are finite; a program needn't handle non-finite values.
Results may differ from the reference program's by a relative error of at most 0.012.
Values may be sent and summed in bfloat16 or wider, within the bound.
A program may use at most 64 MiB of HBM per device.

```python
import math
import jax
import jax.numpy as jnp
from jax import lax

FACE = 768
FACES = 6
CF = 2
ITERS = 3
SIDE = 2
PIECE = 384


def draw_child_maps(key, part):
    order_total = FACES * FACE
    key_diag, key_noise = jax.random.split(jax.random.fold_in(key, 17), 2)
    diagonal = jax.random.uniform(key_diag, (2, order_total, 1), jnp.float32, 0.5, 0.8)
    points = jnp.arange(order_total)
    same_face = points[:, None] // FACE == points[None, :] // FACE
    spread = jnp.where(same_face, 0.3, 0.5) / (2.0 * math.sqrt(FACE))
    noise = jax.random.normal(key_noise, (2, order_total, order_total), jnp.float32)
    full_maps = noise * spread + jnp.where(points[:, None] == points[None, :], diagonal, 0.0)
    blocked = full_maps.reshape(2, FACES, SIDE, PIECE, FACES, SIDE, PIECE).transpose(0, 2, 5, 1, 3, 4, 6)
    return blocked.reshape(2, SIDE * SIDE, FACES * PIECE, FACES * PIECE).astype(jnp.bfloat16)


def setup_inputs(seed: int = 0, part: int = 0) -> dict:
    seeds = jax.random.split(jax.random.key(seed), 3)
    part_keys = jax.random.split(jax.random.fold_in(seeds[2], part), 3)
    return {
        "child_maps": draw_child_maps(jax.random.fold_in(jax.random.fold_in(seeds[2], part), 71), part),
        "face_order": jax.vmap(lambda own: jax.random.permutation(own, FACES))(jax.random.split(part_keys[1], 1 * 2)).reshape((1, 2, FACES)).astype(jnp.int32),
    }


def face_block(matrix, row_face, col_face):
    start_row = (row_face * FACE).astype(jnp.int32)
    start_col = (col_face * FACE).astype(jnp.int32)
    return lax.dynamic_slice(matrix, (start_row, start_col), (FACE, FACE))

def reference(child_maps, face_order):
    order_total = FACES * FACE
    full_maps = child_maps.reshape(2, SIDE, SIDE, FACES, PIECE, FACES, PIECE).transpose(0, 3, 1, 4, 5, 2, 6).reshape(2, order_total, order_total)
    face_list = face_order[0]
    shared, columns, exterior = ([], [], [])
    for child in range(2):
        matrix = full_maps[child]
        own_face = face_list[child, 0]
        shared.append(face_block(matrix, own_face, own_face))
        columns.append(jnp.concatenate([face_block(matrix, own_face, face_list[child, 1 + number]) for number in range(CF)], axis=1))
        exterior.append(jnp.concatenate([face_block(matrix, face_list[child, 1 + number], own_face) for number in range(FACES - 1)], axis=0))
    series, coupled = ([], [])
    for child in range(2):
        partner = 1 - child
        powers = jnp.dot(shared[child], shared[partner], preferred_element_type=jnp.float32).astype(jnp.bfloat16)
        current = columns[child]
        for sweep in range(ITERS):
            current = (current.astype(jnp.float32) + jnp.dot(powers, current, preferred_element_type=jnp.float32)).astype(jnp.bfloat16)
            if sweep < ITERS - 1:
                powers = jnp.dot(powers, powers, preferred_element_type=jnp.float32).astype(jnp.bfloat16)
        series.append(current)
        coupled.append(jnp.dot(shared[partner], current, preferred_element_type=jnp.float32).astype(jnp.bfloat16))
    factors = [jnp.concatenate([coupled[0], series[1]], axis=1), jnp.concatenate([series[0], coupled[1]], axis=1)]
    scaling = math.sqrt(FACE)
    updates = jnp.stack([(jnp.dot(exterior[child], factors[child], preferred_element_type=jnp.float32) * scaling).astype(jnp.bfloat16) for child in range(2)])
    blocked = updates.reshape(2, FACES - 1, SIDE, PIECE, 2 * CF, SIDE, PIECE).transpose(0, 2, 5, 1, 3, 4, 6)
    return blocked.reshape(2, SIDE * SIDE, (FACES - 1) * PIECE, 2 * CF * PIECE)
```

```python
import functools
import math

import jax
import jax.numpy as jnp
from jax import lax
from jax.experimental import pallas as pl
from jax.experimental.pallas import tpu as pltpu
from jax.sharding import PartitionSpec as P

FACE = 768
FACES = 6
CF = 2
ITERS = 3
MESH = pl.DeviceIdType.MESH
VMEM_LIMIT = 56 * 1024 * 1024


def extract_kernel(piece, order_ref, maps_ref, shared_ref, window_ref, exterior_ref, sems):
    child = lax.axis_index("pair")
    own = order_ref[0, child, 0]

    def block(row_face, col_face):
        rows = pl.ds(pl.multiple_of(row_face * piece, piece), piece)
        cols = pl.ds(pl.multiple_of(col_face * piece, piece), piece)
        return maps_ref.at[0, 0, rows, cols]

    copies = [pltpu.make_async_copy(block(own, own), shared_ref, sems.at[0])]
    for number in range(CF):
        copies.append(
            pltpu.make_async_copy(
                block(own, order_ref[0, child, 1 + number]),
                window_ref.at[:, pl.ds(number * piece, piece)],
                sems.at[1 + number],
            )
        )
    for number in range(FACES - 1):
        copies.append(
            pltpu.make_async_copy(
                block(order_ref[0, child, 1 + number], own),
                exterior_ref.at[pl.ds(number * piece, piece)],
                sems.at[1 + CF + number],
            )
        )
    for copy in copies:
        copy.start()
    for copy in copies:
        copy.wait()


def extract(child_maps, face_order, piece):
    shapes = ((piece, piece), (piece, CF * piece), ((FACES - 1) * piece, piece))
    if piece % 128 == 0:
        return pl.pallas_call(
            functools.partial(extract_kernel, piece),
            out_shape=[pltpu.VMEM(shape, child_maps.dtype) for shape in shapes],
            in_specs=[
                pl.BlockSpec(memory_space=pltpu.SMEM),
                pl.BlockSpec(memory_space=pltpu.HBM),
            ],
            out_specs=[pl.BlockSpec(memory_space=pltpu.VMEM)] * 3,
            scratch_shapes=[pltpu.SemaphoreType.DMA((CF + FACES,))],
            name="cut_faces",
        )(face_order, child_maps)
    faces = lax.dynamic_index_in_dim(face_order[0], lax.axis_index("pair"), 0, keepdims=False)
    tile = child_maps[0, 0]

    def block(row_face, col_face):
        return lax.dynamic_slice(tile, (row_face * piece, col_face * piece), (piece, piece))

    window = [block(faces[0], faces[1 + number]) for number in range(CF)]
    exterior = [block(faces[1 + number], faces[0]) for number in range(FACES - 1)]
    return (
        block(faces[0], faces[0]),
        jnp.concatenate(window, axis=1),
        jnp.concatenate(exterior, axis=0),
    )


def matmul(dst, left, right, rows, base=None):
    total = left.shape[0]

    @pl.loop(0, total // rows)
    def _(step):
        at = pl.ds(pl.multiple_of(step * rows, rows), rows)
        value = jnp.dot(left[at, :], right[...], preferred_element_type=jnp.float32)
        if base is not None:
            value = base[at, :].astype(jnp.float32) + value
        dst[at, :] = value.astype(dst.dtype)


def merge_kernel(
    side,
    piece,
    shared_ref,
    window_ref,
    exterior_ref,
    out_ref,
    mine,
    other,
    left,
    right,
    power,
    column,
    series,
    factor,
    rows_all,
    s_send,
    s_recv,
    w_send,
    w_recv,
    e_send,
    e_recv,
    f_send,
    f_recv,
    x_send,
    x_recv,
    l_sem,
):
    count = side * side
    faces = FACES - 1
    child = lax.axis_index("pair")
    tile = lax.axis_index("tile")
    grid_row = tile // side
    grid_col = lax.rem(tile, side)
    partner = {"pair": 1 - child}

    def peer(distance):
        return lax.rem(tile + distance, count)

    def row_peer(distance):
        return lax.rem(grid_row + distance, side)

    def col_peer(distance):
        return lax.rem(grid_col + distance, side)

    barrier = pltpu.get_barrier_semaphore()
    for distance in range(1, count):
        pl.semaphore_signal(
            barrier, inc=1, device_id={"tile": peer(distance)}, device_id_type=MESH
        )
    pl.semaphore_signal(barrier, inc=1, device_id=partner, device_id_type=MESH)
    pl.semaphore_wait(barrier, count)

    def remote(src, dst, send, recv, target):
        return pltpu.make_async_remote_copy(
            src_ref=src,
            dst_ref=dst,
            send_sem=send,
            recv_sem=recv,
            device_id=target,
            device_id_type=MESH,
        )

    s_copies = {}
    for distance in range(1, count):
        s_copies[distance] = remote(
            shared_ref,
            mine.at[tile],
            s_send.at[distance],
            s_recv.at[distance],
            {"tile": peer(distance)},
        )
    w_copies = {}
    for distance in range(1, side):
        w_copies[distance] = remote(
            window_ref,
            column.at[grid_row],
            w_send.at[distance],
            w_recv.at[distance],
            {"tile": row_peer(distance) * side + grid_col},
        )
    e_copies = {}
    for face in range(faces):
        for distance in range(1, side):
            e_copies[face, distance] = remote(
                exterior_ref.at[pl.ds(face * piece, piece)],
                rows_all.at[face, grid_col],
                e_send.at[face, distance],
                e_recv.at[face, distance],
                {"tile": grid_row * side + col_peer(distance)},
            )
    own_forward = remote(
        shared_ref, other.at[tile], f_send.at[0], f_recv.at[0], partner
    )
    for copy in s_copies.values():
        copy.start()
    own_forward.start()
    for copy in w_copies.values():
        copy.start()

    locals_ = [
        pltpu.make_async_copy(shared_ref, mine.at[tile], l_sem.at[0]),
        pltpu.make_async_copy(window_ref, column.at[grid_row], l_sem.at[1]),
    ]
    for face in range(faces):
        locals_.append(
            pltpu.make_async_copy(
                exterior_ref.at[pl.ds(face * piece, piece)],
                rows_all.at[face, grid_col],
                l_sem.at[2 + face],
            )
        )
    for copy in locals_:
        copy.start()

    forwards = [own_forward]
    for distance in range(1, count):
        s_copies[distance].wait_recv()
        source = lax.rem(tile + count - distance, count)
        forward = remote(
            mine.at[source],
            other.at[source],
            f_send.at[distance],
            f_recv.at[distance],
            partner,
        )
        forward.start()
        forwards.append(forward)
    for copy in e_copies.values():
        copy.start()
    for forward in forwards:
        forward.wait_recv()
    for copy in locals_:
        copy.wait()

    for number in range(count):
        at_row, at_col = number // side * piece, number % side * piece
        left[at_row : at_row + piece, at_col : at_col + piece] = mine[number]
        right[at_row : at_row + piece, at_col : at_col + piece] = other[number]

    block = math.gcd(left.shape[0], 256)
    matmul(power.at[0], left, right, block)
    for sweep in range(1, ITERS):
        matmul(power.at[sweep], power.at[sweep - 1], power.at[sweep - 1], block)
    for distance in range(1, side):
        w_copies[distance].wait_recv()
    for number in range(side):
        series[0, number * piece : (number + 1) * piece, :] = column[number]
    now = 0
    for sweep in range(ITERS):
        matmul(series.at[1 - now], power.at[sweep], series.at[now], block, base=series.at[now])
        now = 1 - now
    exchange = remote(series.at[now], factor.at[child], x_send, x_recv, partner)
    exchange.start()
    matmul(factor.at[child], right, series.at[now], block)
    exchange.wait_recv()

    half = CF * piece
    scale = math.sqrt(FACE)
    sub = 2
    step_rows = piece // sub
    for face in range(faces):
        for distance in range(1, side):
            e_copies[face, distance].wait_recv()

        @pl.loop(0, sub)
        def _(step, face=face):
            at = pl.ds(pl.multiple_of(step * step_rows, step_rows), step_rows)
            rows = jnp.concatenate([rows_all[face, k, at, :] for k in range(side)], axis=1)
            to = pl.ds(pl.multiple_of(face * piece + step * step_rows, step_rows), step_rows)
            for part in range(2):
                value = jnp.dot(rows, factor[part], preferred_element_type=jnp.float32) * scale
                out_ref[to, part * half : (part + 1) * half] = value.astype(out_ref.dtype)

    for copy in [*s_copies.values(), *w_copies.values(), *e_copies.values(), *forwards, exchange]:
        copy.wait_send()


def local(child_maps, face_order):
    side = math.isqrt(lax.axis_size("tile"))
    count = side * side
    piece = child_maps.shape[2] // FACES
    order = side * piece
    dtype = child_maps.dtype
    faces = FACES - 1
    shared, window, exterior = extract(child_maps, face_order, piece)
    dma = pltpu.SemaphoreType.DMA
    update = pl.pallas_call(
        functools.partial(merge_kernel, side, piece),
        out_shape=pltpu.VMEM((faces * piece, 2 * CF * piece), dtype),
        in_specs=[pl.BlockSpec(memory_space=pl.ANY)] * 3,
        out_specs=pl.BlockSpec(memory_space=pltpu.VMEM),
        scratch_shapes=[
            pltpu.VMEM((count, piece, piece), dtype),
            pltpu.VMEM((count, piece, piece), dtype),
            pltpu.VMEM((order, order), dtype),
            pltpu.VMEM((order, order), dtype),
            pltpu.VMEM((ITERS, order, order), dtype),
            pltpu.VMEM((side, piece, CF * piece), dtype),
            pltpu.VMEM((2, order, CF * piece), dtype),
            pltpu.VMEM((2, order, CF * piece), dtype),
            pltpu.VMEM((faces, side, piece, piece), dtype),
            dma((count,)),
            dma((count,)),
            dma((side,)),
            dma((side,)),
            dma((faces, side)),
            dma((faces, side)),
            dma((count,)),
            dma((count,)),
            dma(()),
            dma(()),
            dma((2 + faces,)),
        ],
        compiler_params=pltpu.CompilerParams(
            collective_id=0, has_side_effects=True, vmem_limit_bytes=VMEM_LIMIT
        ),
        name="merge",
    )(shared, window, exterior)
    return update[None, None]


def solution(mesh):
    return jax.shard_map(
        local,
        mesh=mesh,
        in_specs=(P("pair", ("box", "tile"), None, None), P("box", None, None)),
        out_specs=P("pair", ("box", "tile"), None, None),
        check_vma=False,
    )
```

```python
import functools
import math

import jax
import jax.numpy as jnp
from jax import lax
from jax.experimental import pallas as pl
from jax.experimental.pallas import tpu as pltpu
from jax.sharding import PartitionSpec as P

FACE = 768
FACES = 6
CF = 2
ITERS = 3
MESH = pl.DeviceIdType.MESH
VMEM_LIMIT = 32 * 1024 * 1024


def extract_kernel(piece, order_ref, maps_ref, shared_ref, window_ref, exterior_ref, sems):
    child = lax.axis_index("pair")
    own = order_ref[0, child, 0]

    def block(row_face, col_face):
        rows = pl.ds(pl.multiple_of(row_face * piece, piece), piece)
        cols = pl.ds(pl.multiple_of(col_face * piece, piece), piece)
        return maps_ref.at[0, 0, rows, cols]

    copies = [pltpu.make_async_copy(block(own, own), shared_ref, sems.at[0])]
    for number in range(CF):
        copies.append(
            pltpu.make_async_copy(
                block(own, order_ref[0, child, 1 + number]),
                window_ref.at[:, pl.ds(number * piece, piece)],
                sems.at[1 + number],
            )
        )
    for number in range(FACES - 1):
        copies.append(
            pltpu.make_async_copy(
                block(order_ref[0, child, 1 + number], own),
                exterior_ref.at[pl.ds(number * piece, piece)],
                sems.at[1 + CF + number],
            )
        )
    for copy in copies:
        copy.start()
    for copy in copies:
        copy.wait()


def extract(child_maps, face_order, piece):
    shapes = ((piece, piece), (piece, CF * piece), ((FACES - 1) * piece, piece))
    if piece % 128 == 0:
        return pl.pallas_call(
            functools.partial(extract_kernel, piece),
            out_shape=[pltpu.VMEM(shape, child_maps.dtype) for shape in shapes],
            in_specs=[
                pl.BlockSpec(memory_space=pltpu.SMEM),
                pl.BlockSpec(memory_space=pltpu.HBM),
            ],
            out_specs=[pl.BlockSpec(memory_space=pltpu.VMEM)] * 3,
            scratch_shapes=[pltpu.SemaphoreType.DMA((CF + FACES,))],
            name="cut_faces",
        )(face_order, child_maps)
    faces = lax.dynamic_index_in_dim(face_order[0], lax.axis_index("pair"), 0, keepdims=False)
    tile = child_maps[0, 0]

    def block(row_face, col_face):
        return lax.dynamic_slice(tile, (row_face * piece, col_face * piece), (piece, piece))

    window = [block(faces[0], faces[1 + number]) for number in range(CF)]
    exterior = [block(faces[1 + number], faces[0]) for number in range(FACES - 1)]
    return (
        block(faces[0], faces[0]),
        jnp.concatenate(window, axis=1),
        jnp.concatenate(exterior, axis=0),
    )


def matmul(dst, left, right, rows, base=None):
    total = left.shape[0]

    @pl.loop(0, total // rows)
    def _(step):
        at = pl.ds(pl.multiple_of(step * rows, rows), rows)
        value = jnp.dot(left[at, :], right[...], preferred_element_type=jnp.float32)
        if base is not None:
            value = base[at, :].astype(jnp.float32) + value
        dst[at, :] = value.astype(dst.dtype)


def merge_kernel(
    side,
    piece,
    shared_ref,
    window_ref,
    exterior_ref,
    out_ref,
    mine,
    other,
    left,
    right,
    power,
    column,
    series,
    factor,
    rows_all,
    s_send,
    s_recv,
    w_send,
    w_recv,
    e_send,
    e_recv,
    f_send,
    f_recv,
    x_send,
    x_recv,
    l_sem,
):
    count = side * side
    faces = FACES - 1
    child = lax.axis_index("pair")
    tile = lax.axis_index("tile")
    grid_row = tile // side
    grid_col = lax.rem(tile, side)
    partner = {"pair": 1 - child}

    def peer(distance):
        return lax.rem(tile + distance, count)

    def row_peer(distance):
        return lax.rem(grid_row + distance, side)

    def col_peer(distance):
        return lax.rem(grid_col + distance, side)

    barrier = pltpu.get_barrier_semaphore()
    for distance in range(1, count):
        pl.semaphore_signal(
            barrier, inc=1, device_id={"tile": peer(distance)}, device_id_type=MESH
        )
    pl.semaphore_signal(barrier, inc=1, device_id=partner, device_id_type=MESH)
    pl.semaphore_wait(barrier, count)

    def remote(src, dst, send, recv, target):
        return pltpu.make_async_remote_copy(
            src_ref=src,
            dst_ref=dst,
            send_sem=send,
            recv_sem=recv,
            device_id=target,
            device_id_type=MESH,
        )

    s_copies = {}
    for distance in range(1, count):
        s_copies[distance] = remote(
            shared_ref,
            mine.at[tile],
            s_send.at[distance],
            s_recv.at[distance],
            {"tile": peer(distance)},
        )
    w_copies = {}
    for distance in range(1, side):
        w_copies[distance] = remote(
            window_ref,
            column.at[grid_row],
            w_send.at[distance],
            w_recv.at[distance],
            {"tile": row_peer(distance) * side + grid_col},
        )
    e_copies = {}
    for face in range(faces):
        for distance in range(1, side):
            e_copies[face, distance] = remote(
                exterior_ref.at[pl.ds(face * piece, piece)],
                rows_all.at[face, grid_col],
                e_send.at[face, distance],
                e_recv.at[face, distance],
                {"tile": grid_row * side + col_peer(distance)},
            )
    own_forward = remote(
        shared_ref, other.at[tile], f_send.at[0], f_recv.at[0], partner
    )
    for copy in s_copies.values():
        copy.start()
    own_forward.start()
    for copy in w_copies.values():
        copy.start()
    for copy in e_copies.values():
        copy.start()

    locals_ = [
        pltpu.make_async_copy(shared_ref, mine.at[tile], l_sem.at[0]),
        pltpu.make_async_copy(window_ref, column.at[grid_row], l_sem.at[1]),
    ]
    for face in range(faces):
        locals_.append(
            pltpu.make_async_copy(
                exterior_ref.at[pl.ds(face * piece, piece)],
                rows_all.at[face, grid_col],
                l_sem.at[2 + face],
            )
        )
    for copy in locals_:
        copy.start()

    forwards = [own_forward]
    for distance in range(1, count):
        s_copies[distance].wait_recv()
        source = lax.rem(tile + count - distance, count)
        forward = remote(
            mine.at[source],
            other.at[source],
            f_send.at[distance],
            f_recv.at[distance],
            partner,
        )
        forward.start()
        forwards.append(forward)
    for forward in forwards:
        forward.wait_recv()
    for copy in locals_:
        copy.wait()

    for number in range(count):
        at_row, at_col = number // side * piece, number % side * piece
        left[at_row : at_row + piece, at_col : at_col + piece] = mine[number]
        right[at_row : at_row + piece, at_col : at_col + piece] = other[number]

    block = math.gcd(left.shape[0], 256)
    matmul(power.at[0], left, right, block)
    for sweep in range(1, ITERS):
        matmul(power.at[sweep], power.at[sweep - 1], power.at[sweep - 1], block)
    for distance in range(1, side):
        w_copies[distance].wait_recv()
    for number in range(side):
        series[0, number * piece : (number + 1) * piece, :] = column[number]
    now = 0
    for sweep in range(ITERS):
        matmul(series.at[1 - now], power.at[sweep], series.at[now], block, base=series.at[now])
        now = 1 - now
    exchange = remote(series.at[now], factor.at[child], x_send, x_recv, partner)
    exchange.start()
    matmul(factor.at[child], right, series.at[now], block)
    exchange.wait_recv()

    half = CF * piece
    scale = math.sqrt(FACE)
    sub = 2
    step_rows = piece // sub
    for face in range(faces):
        for distance in range(1, side):
            e_copies[face, distance].wait_recv()

        @pl.loop(0, sub)
        def _(step, face=face):
            at = pl.ds(pl.multiple_of(step * step_rows, step_rows), step_rows)
            rows = jnp.concatenate([rows_all[face, k, at, :] for k in range(side)], axis=1)
            to = pl.ds(pl.multiple_of(face * piece + step * step_rows, step_rows), step_rows)
            for part in range(2):
                value = jnp.dot(rows, factor[part], preferred_element_type=jnp.float32) * scale
                out_ref[to, part * half : (part + 1) * half] = value.astype(out_ref.dtype)

    for copy in [*s_copies.values(), *w_copies.values(), *e_copies.values(), *forwards, exchange]:
        copy.wait_send()


def local(child_maps, face_order):
    side = math.isqrt(lax.axis_size("tile"))
    count = side * side
    piece = child_maps.shape[2] // FACES
    order = side * piece
    dtype = child_maps.dtype
    faces = FACES - 1
    shared, window, exterior = extract(child_maps, face_order, piece)
    dma = pltpu.SemaphoreType.DMA
    update = pl.pallas_call(
        functools.partial(merge_kernel, side, piece),
        out_shape=pltpu.VMEM((faces * piece, 2 * CF * piece), dtype),
        in_specs=[pl.BlockSpec(memory_space=pl.ANY)] * 3,
        out_specs=pl.BlockSpec(memory_space=pltpu.VMEM),
        scratch_shapes=[
            pltpu.VMEM((count, piece, piece), dtype),
            pltpu.VMEM((count, piece, piece), dtype),
            pltpu.VMEM((order, order), dtype),
            pltpu.VMEM((order, order), dtype),
            pltpu.VMEM((ITERS, order, order), dtype),
            pltpu.VMEM((side, piece, CF * piece), dtype),
            pltpu.VMEM((2, order, CF * piece), dtype),
            pltpu.VMEM((2, order, CF * piece), dtype),
            pltpu.VMEM((faces, side, piece, piece), dtype),
            dma((count,)),
            dma((count,)),
            dma((side,)),
            dma((side,)),
            dma((faces, side)),
            dma((faces, side)),
            dma((count,)),
            dma((count,)),
            dma(()),
            dma(()),
            dma((2 + faces,)),
        ],
        compiler_params=pltpu.CompilerParams(
            collective_id=0, has_side_effects=True, vmem_limit_bytes=VMEM_LIMIT
        ),
        name="merge",
    )(shared, window, exterior)
    return update[None, None]


def solution(mesh):
    return jax.shard_map(
        local,
        mesh=mesh,
        in_specs=(P("pair", ("box", "tile"), None, None), P("box", None, None)),
        out_specs=P("pair", ("box", "tile"), None, None),
        check_vma=False,
    )
```

```python
import functools
import math

import jax
import jax.numpy as jnp
from jax import lax
from jax.experimental import pallas as pl
from jax.experimental.pallas import tpu as pltpu
from jax.sharding import PartitionSpec as P

FACE = 768
FACES = 6
CF = 2
ITERS = 3
MESH = pl.DeviceIdType.MESH
VMEM_LIMIT = 32 * 1024 * 1024
FINISH_LIMIT = 16 * 1024 * 1024


def extract_kernel(piece, order_ref, maps_ref, shared_ref, window_ref, exterior_ref, sems):
    child = lax.axis_index("pair")
    own = order_ref[0, child, 0]

    def block(row_face, col_face):
        rows = pl.ds(pl.multiple_of(row_face * piece, piece), piece)
        cols = pl.ds(pl.multiple_of(col_face * piece, piece), piece)
        return maps_ref.at[0, 0, rows, cols]

    copies = [pltpu.make_async_copy(block(own, own), shared_ref, sems.at[0])]
    for number in range(CF):
        copies.append(
            pltpu.make_async_copy(
                block(own, order_ref[0, child, 1 + number]),
                window_ref.at[:, pl.ds(number * piece, piece)],
                sems.at[1 + number],
            )
        )
    for number in range(FACES - 1):
        copies.append(
            pltpu.make_async_copy(
                block(order_ref[0, child, 1 + number], own),
                exterior_ref.at[pl.ds(number * piece, piece)],
                sems.at[1 + CF + number],
            )
        )
    for copy in copies:
        copy.start()
    for copy in copies:
        copy.wait()


def extract(child_maps, face_order, piece):
    shapes = ((piece, piece), (piece, CF * piece), ((FACES - 1) * piece, piece))
    if piece % 128 == 0:
        return pl.pallas_call(
            functools.partial(extract_kernel, piece),
            out_shape=[pltpu.VMEM(shape, child_maps.dtype) for shape in shapes],
            in_specs=[
                pl.BlockSpec(memory_space=pltpu.SMEM),
                pl.BlockSpec(memory_space=pltpu.HBM),
            ],
            out_specs=[pl.BlockSpec(memory_space=pltpu.VMEM)] * 3,
            scratch_shapes=[pltpu.SemaphoreType.DMA((CF + FACES,))],
            name="cut_faces",
        )(face_order, child_maps)
    faces = lax.dynamic_index_in_dim(face_order[0], lax.axis_index("pair"), 0, keepdims=False)
    tile = child_maps[0, 0]

    def block(row_face, col_face):
        return lax.dynamic_slice(tile, (row_face * piece, col_face * piece), (piece, piece))

    window = [block(faces[0], faces[1 + number]) for number in range(CF)]
    exterior = [block(faces[1 + number], faces[0]) for number in range(FACES - 1)]
    return (
        block(faces[0], faces[0]),
        jnp.concatenate(window, axis=1),
        jnp.concatenate(exterior, axis=0),
    )


def matmul(dst, left, right, rows, base=None):
    total = left.shape[0]

    @pl.loop(0, total // rows)
    def _(step):
        at = pl.ds(pl.multiple_of(step * rows, rows), rows)
        value = jnp.dot(left[at, :], right[...], preferred_element_type=jnp.float32)
        if base is not None:
            value = base[at, :].astype(jnp.float32) + value
        dst[at, :] = value.astype(dst.dtype)


def final_rows(rows_ref, factor, dst, base, first, count):
    half = factor.shape[2]
    at = pl.ds(first, count)
    rows = jnp.concatenate([rows_ref[k, at, :] for k in range(rows_ref.shape[0])], axis=1)
    for part in range(2):
        value = jnp.dot(rows, factor[part], preferred_element_type=jnp.float32)
        value = value * math.sqrt(FACE)
        dst[pl.ds(base + first, count), part * half : (part + 1) * half] = value.astype(dst.dtype)


def finish_kernel(side, piece, held_ref, rows_ref, factor, out_ref, hold, sems):
    parts = 2
    size = piece // parts
    start = held_ref.shape[0]
    copies = []
    for face in range(FACES - 2):
        at = pl.ds(face * piece, piece)
        copies.append(pltpu.make_async_copy(held_ref.at[at], out_ref.at[at], sems.at[parts + face]))
        copies[-1].start()
    for part in range(parts):
        final_rows(rows_ref, factor, hold, 0, part * size, size)
        copy = pltpu.make_async_copy(
            hold.at[pl.ds(part * size, size)],
            out_ref.at[pl.ds(start + part * size, size)],
            sems.at[part],
        )
        copy.start()
        copies.append(copy)
    for copy in copies:
        copy.wait()


def merge_kernel(
    side,
    piece,
    shared_ref,
    window_ref,
    exterior_ref,
    out_ref,
    rows_last,
    factor,
    mine,
    other,
    left,
    right,
    power,
    column,
    series,
    rows_all,
    s_send,
    s_recv,
    w_send,
    w_recv,
    e_send,
    e_recv,
    f_send,
    f_recv,
    x_send,
    x_recv,
    l_sem,
):
    count = side * side
    faces = FACES - 1
    child = lax.axis_index("pair")
    tile = lax.axis_index("tile")
    grid_row = tile // side
    grid_col = lax.rem(tile, side)
    partner = {"pair": 1 - child}

    def peer(distance):
        return lax.rem(tile + distance, count)

    def row_peer(distance):
        return lax.rem(grid_row + distance, side)

    def col_peer(distance):
        return lax.rem(grid_col + distance, side)

    barrier = pltpu.get_barrier_semaphore()
    for distance in range(1, count):
        pl.semaphore_signal(
            barrier, inc=1, device_id={"tile": peer(distance)}, device_id_type=MESH
        )
    pl.semaphore_signal(barrier, inc=1, device_id=partner, device_id_type=MESH)
    pl.semaphore_wait(barrier, count)

    def rows_at(face):
        return rows_all.at[face] if face < faces - 1 else rows_last

    def remote(src, dst, send, recv, target):
        return pltpu.make_async_remote_copy(
            src_ref=src,
            dst_ref=dst,
            send_sem=send,
            recv_sem=recv,
            device_id=target,
            device_id_type=MESH,
        )

    s_copies = {}
    for distance in range(1, count):
        s_copies[distance] = remote(
            shared_ref,
            mine.at[tile],
            s_send.at[distance],
            s_recv.at[distance],
            {"tile": peer(distance)},
        )
    w_copies = {}
    for distance in range(1, side):
        w_copies[distance] = remote(
            window_ref,
            column.at[grid_row],
            w_send.at[distance],
            w_recv.at[distance],
            {"tile": row_peer(distance) * side + grid_col},
        )
    e_copies = {}
    for face in range(faces):
        for distance in range(1, side):
            e_copies[face, distance] = remote(
                exterior_ref.at[pl.ds(face * piece, piece)],
                rows_at(face).at[grid_col],
                e_send.at[face, distance],
                e_recv.at[face, distance],
                {"tile": grid_row * side + col_peer(distance)},
            )
    own_forward = remote(
        shared_ref, other.at[tile], f_send.at[0], f_recv.at[0], partner
    )
    for copy in s_copies.values():
        copy.start()
    own_forward.start()
    for copy in w_copies.values():
        copy.start()
    for copy in e_copies.values():
        copy.start()

    locals_ = [
        pltpu.make_async_copy(shared_ref, mine.at[tile], l_sem.at[0]),
        pltpu.make_async_copy(window_ref, column.at[grid_row], l_sem.at[1]),
    ]
    for face in range(faces):
        locals_.append(
            pltpu.make_async_copy(
                exterior_ref.at[pl.ds(face * piece, piece)],
                rows_at(face).at[grid_col],
                l_sem.at[2 + face],
            )
        )
    for copy in locals_:
        copy.start()

    forwards = [own_forward]
    for distance in range(1, count):
        s_copies[distance].wait_recv()
        source = lax.rem(tile + count - distance, count)
        forward = remote(
            mine.at[source],
            other.at[source],
            f_send.at[distance],
            f_recv.at[distance],
            partner,
        )
        forward.start()
        forwards.append(forward)
    for forward in forwards:
        forward.wait_recv()
    for copy in locals_:
        copy.wait()

    for number in range(count):
        at_row, at_col = number // side * piece, number % side * piece
        left[at_row : at_row + piece, at_col : at_col + piece] = mine[number]
        right[at_row : at_row + piece, at_col : at_col + piece] = other[number]

    block = math.gcd(left.shape[0], 256)
    matmul(power.at[0], left, right, block)
    for sweep in range(1, ITERS):
        matmul(power.at[sweep], power.at[sweep - 1], power.at[sweep - 1], block)
    for distance in range(1, side):
        w_copies[distance].wait_recv()
    for number in range(side):
        series[0, number * piece : (number + 1) * piece, :] = column[number]
    now = 0
    for sweep in range(ITERS):
        matmul(series.at[1 - now], power.at[sweep], series.at[now], block, base=series.at[now])
        now = 1 - now
    exchange = remote(series.at[now], factor.at[child], x_send, x_recv, partner)
    exchange.start()
    matmul(factor.at[child], right, series.at[now], block)
    exchange.wait_recv()

    for face in range(faces - 1):
        for distance in range(1, side):
            e_copies[face, distance].wait_recv()
        final_rows(rows_all.at[face], factor, out_ref, face * piece, 0, piece)
    for distance in range(1, side):
        e_copies[faces - 1, distance].wait_recv()

    for copy in [*s_copies.values(), *w_copies.values(), *e_copies.values(), *forwards, exchange]:
        copy.wait_send()


def local(child_maps, face_order):
    side = math.isqrt(lax.axis_size("tile"))
    count = side * side
    piece = child_maps.shape[2] // FACES
    order = side * piece
    dtype = child_maps.dtype
    faces = FACES - 1
    shared, window, exterior = extract(child_maps, face_order, piece)
    dma = pltpu.SemaphoreType.DMA
    held, rows_last, factor = pl.pallas_call(
        functools.partial(merge_kernel, side, piece),
        out_shape=[
            pltpu.VMEM(((faces - 1) * piece, 2 * CF * piece), dtype),
            pltpu.VMEM((side, piece, piece), dtype),
            pltpu.VMEM((2, order, CF * piece), dtype),
        ],
        in_specs=[pl.BlockSpec(memory_space=pl.ANY)] * 3,
        out_specs=[
            pl.BlockSpec(memory_space=pltpu.VMEM),
            pl.BlockSpec(memory_space=pltpu.VMEM),
            pl.BlockSpec(memory_space=pltpu.VMEM),
        ],
        scratch_shapes=[
            pltpu.VMEM((count, piece, piece), dtype),
            pltpu.VMEM((count, piece, piece), dtype),
            pltpu.VMEM((order, order), dtype),
            pltpu.VMEM((order, order), dtype),
            pltpu.VMEM((ITERS, order, order), dtype),
            pltpu.VMEM((side, piece, CF * piece), dtype),
            pltpu.VMEM((2, order, CF * piece), dtype),
            pltpu.VMEM((faces - 1, side, piece, piece), dtype),
            dma((count,)),
            dma((count,)),
            dma((side,)),
            dma((side,)),
            dma((faces, side)),
            dma((faces, side)),
            dma((count,)),
            dma((count,)),
            dma(()),
            dma(()),
            dma((2 + faces,)),
        ],
        compiler_params=pltpu.CompilerParams(
            collective_id=0, has_side_effects=True, vmem_limit_bytes=VMEM_LIMIT
        ),
        name="merge",
    )(shared, window, exterior)
    update = pl.pallas_call(
        functools.partial(finish_kernel, side, piece),
        out_shape=jax.ShapeDtypeStruct((faces * piece, 2 * CF * piece), dtype),
        in_specs=[
            pl.BlockSpec(memory_space=pl.ANY),
            pl.BlockSpec(memory_space=pltpu.VMEM),
            pl.BlockSpec(memory_space=pltpu.VMEM),
        ],
        out_specs=pl.BlockSpec(memory_space=pl.ANY),
        scratch_shapes=[
            pltpu.VMEM((piece, 2 * CF * piece), dtype),
            dma((FACES,)),
        ],
        compiler_params=pltpu.CompilerParams(vmem_limit_bytes=FINISH_LIMIT),
        name="finish",
    )(held, rows_last, factor)
    return update[None, None]


def solution(mesh):
    return jax.shard_map(
        local,
        mesh=mesh,
        in_specs=(P("pair", ("box", "tile"), None, None), P("box", None, None)),
        out_specs=P("pair", ("box", "tile"), None, None),
        check_vma=False,
    )
```

```python
import functools
import math

import jax
import jax.numpy as jnp
from jax import lax
from jax.experimental import pallas as pl
from jax.experimental.pallas import tpu as pltpu
from jax.sharding import PartitionSpec as P

FACE = 768
FACES = 6
CF = 2
ITERS = 3
MESH = pl.DeviceIdType.MESH
VMEM_LIMIT = 32 * 1024 * 1024
FINISH_LIMIT = 16 * 1024 * 1024


def extract_kernel(piece, order_ref, maps_ref, shared_ref, window_ref, exterior_ref, sems):
    child = lax.axis_index("pair")
    own = order_ref[0, child, 0]

    def block(row_face, col_face):
        rows = pl.ds(pl.multiple_of(row_face * piece, piece), piece)
        cols = pl.ds(pl.multiple_of(col_face * piece, piece), piece)
        return maps_ref.at[0, 0, rows, cols]

    copies = [pltpu.make_async_copy(block(own, own), shared_ref, sems.at[0])]
    for number in range(CF):
        copies.append(
            pltpu.make_async_copy(
                block(own, order_ref[0, child, 1 + number]),
                window_ref.at[:, pl.ds(number * piece, piece)],
                sems.at[1 + number],
            )
        )
    for number in range(FACES - 1):
        copies.append(
            pltpu.make_async_copy(
                block(order_ref[0, child, 1 + number], own),
                exterior_ref.at[pl.ds(number * piece, piece)],
                sems.at[1 + CF + number],
            )
        )
    for copy in copies:
        copy.start()
    for copy in copies:
        copy.wait()


def extract(child_maps, face_order, piece):
    shapes = ((piece, piece), (piece, CF * piece), ((FACES - 1) * piece, piece))
    if piece % 128 == 0:
        return pl.pallas_call(
            functools.partial(extract_kernel, piece),
            out_shape=[pltpu.VMEM(shape, child_maps.dtype) for shape in shapes],
            in_specs=[
                pl.BlockSpec(memory_space=pltpu.SMEM),
                pl.BlockSpec(memory_space=pltpu.HBM),
            ],
            out_specs=[pl.BlockSpec(memory_space=pltpu.VMEM)] * 3,
            scratch_shapes=[pltpu.SemaphoreType.DMA((CF + FACES,))],
            name="cut_faces",
        )(face_order, child_maps)
    faces = lax.dynamic_index_in_dim(face_order[0], lax.axis_index("pair"), 0, keepdims=False)
    tile = child_maps[0, 0]

    def block(row_face, col_face):
        return lax.dynamic_slice(tile, (row_face * piece, col_face * piece), (piece, piece))

    window = [block(faces[0], faces[1 + number]) for number in range(CF)]
    exterior = [block(faces[1 + number], faces[0]) for number in range(FACES - 1)]
    return (
        block(faces[0], faces[0]),
        jnp.concatenate(window, axis=1),
        jnp.concatenate(exterior, axis=0),
    )


def matmul(dst, left, right, rows, base=None):
    total = left.shape[0]

    @pl.loop(0, total // rows)
    def _(step):
        at = pl.ds(pl.multiple_of(step * rows, rows), rows)
        value = jnp.dot(left[at, :], right[...], preferred_element_type=jnp.float32)
        if base is not None:
            value = base[at, :].astype(jnp.float32) + value
        dst[at, :] = value.astype(dst.dtype)


def final_rows(rows_ref, factor, dst, base, first, count):
    half = factor.shape[2]
    at = pl.ds(first, count)
    rows = jnp.concatenate([rows_ref[k, at, :] for k in range(rows_ref.shape[0])], axis=1)
    for part in range(2):
        value = jnp.dot(rows, factor[part], preferred_element_type=jnp.float32)
        value = value * math.sqrt(FACE)
        dst[pl.ds(base + first, count), part * half : (part + 1) * half] = value.astype(dst.dtype)


def finish_kernel(side, piece, held_ref, rows_ref, factor, out_ref, hold, sems):
    parts = 2
    size = piece // parts
    start = held_ref.shape[0]
    copies = []
    for face in range(FACES - 2):
        at = pl.ds(face * piece, piece)
        copies.append(pltpu.make_async_copy(held_ref.at[at], out_ref.at[at], sems.at[parts + face]))
        copies[-1].start()
    for part in range(parts):
        final_rows(rows_ref, factor, hold, 0, part * size, size)
        copy = pltpu.make_async_copy(
            hold.at[pl.ds(part * size, size)],
            out_ref.at[pl.ds(start + part * size, size)],
            sems.at[part],
        )
        copy.start()
        copies.append(copy)
    for copy in copies:
        copy.wait()


def merge_kernel(
    side,
    piece,
    shared_ref,
    window_ref,
    exterior_ref,
    out_ref,
    rows_last,
    factor,
    mine,
    other,
    left,
    right,
    power,
    column,
    series,
    rows_all,
    s_send,
    s_recv,
    w_send,
    w_recv,
    e_send,
    e_recv,
    f_send,
    f_recv,
    x_send,
    x_recv,
    l_sem,
):
    count = side * side
    faces = FACES - 1
    child = lax.axis_index("pair")
    tile = lax.axis_index("tile")
    grid_row = tile // side
    grid_col = lax.rem(tile, side)
    partner = {"pair": 1 - child}

    def peer(distance):
        return lax.rem(tile + distance, count)

    def grid_peer(distance):
        row = lax.rem(grid_row + distance // side, side)
        return row * side + lax.rem(grid_col + distance % side, side)

    def grid_source(distance):
        row = lax.rem(grid_row + side - distance // side, side)
        return row * side + lax.rem(grid_col + side - distance % side, side)

    def row_peer(distance):
        return lax.rem(grid_row + distance, side)

    def col_peer(distance):
        return lax.rem(grid_col + distance, side)

    barrier = pltpu.get_barrier_semaphore()
    for distance in range(1, count):
        pl.semaphore_signal(
            barrier, inc=1, device_id={"tile": peer(distance)}, device_id_type=MESH
        )
    pl.semaphore_signal(barrier, inc=1, device_id=partner, device_id_type=MESH)
    pl.semaphore_wait(barrier, count)

    def rows_at(face):
        return rows_all.at[face] if face < faces - 1 else rows_last

    def remote(src, dst, send, recv, target):
        return pltpu.make_async_remote_copy(
            src_ref=src,
            dst_ref=dst,
            send_sem=send,
            recv_sem=recv,
            device_id=target,
            device_id_type=MESH,
        )

    s_copies = {}
    for distance in range(1, count):
        s_copies[distance] = remote(
            shared_ref,
            mine.at[tile],
            s_send.at[distance],
            s_recv.at[distance],
            {"tile": grid_peer(distance)},
        )
    w_copies = {}
    for distance in range(1, side):
        w_copies[distance] = remote(
            window_ref,
            column.at[grid_row],
            w_send.at[distance],
            w_recv.at[distance],
            {"tile": row_peer(distance) * side + grid_col},
        )
    e_copies = {}
    for face in range(faces):
        for distance in range(1, side):
            e_copies[face, distance] = remote(
                exterior_ref.at[pl.ds(face * piece, piece)],
                rows_at(face).at[grid_col],
                e_send.at[face, distance],
                e_recv.at[face, distance],
                {"tile": grid_row * side + col_peer(distance)},
            )
    own_forward = remote(
        shared_ref, other.at[tile], f_send.at[0], f_recv.at[0], partner
    )
    for copy in s_copies.values():
        copy.start()
    own_forward.start()
    for copy in w_copies.values():
        copy.start()
    for copy in e_copies.values():
        copy.start()

    locals_ = [
        pltpu.make_async_copy(shared_ref, mine.at[tile], l_sem.at[0]),
        pltpu.make_async_copy(window_ref, column.at[grid_row], l_sem.at[1]),
    ]
    for face in range(faces):
        locals_.append(
            pltpu.make_async_copy(
                exterior_ref.at[pl.ds(face * piece, piece)],
                rows_at(face).at[grid_col],
                l_sem.at[2 + face],
            )
        )
    for copy in locals_:
        copy.start()

    forwards = [own_forward]
    for distance in range(1, count):
        s_copies[distance].wait_recv()
        source = grid_source(distance)
        forward = remote(
            mine.at[source],
            other.at[source],
            f_send.at[distance],
            f_recv.at[distance],
            partner,
        )
        forward.start()
        forwards.append(forward)
    for forward in forwards:
        forward.wait_recv()
    for copy in locals_:
        copy.wait()

    for number in range(count):
        at_row, at_col = number // side * piece, number % side * piece
        left[at_row : at_row + piece, at_col : at_col + piece] = mine[number]
        right[at_row : at_row + piece, at_col : at_col + piece] = other[number]

    block = math.gcd(left.shape[0], 256)
    matmul(power.at[0], left, right, block)
    for sweep in range(1, ITERS):
        matmul(power.at[sweep], power.at[sweep - 1], power.at[sweep - 1], block)
    for distance in range(1, side):
        w_copies[distance].wait_recv()
    for number in range(side):
        series[0, number * piece : (number + 1) * piece, :] = column[number]
    now = 0
    for sweep in range(ITERS):
        matmul(series.at[1 - now], power.at[sweep], series.at[now], block, base=series.at[now])
        now = 1 - now
    exchange = remote(series.at[now], factor.at[child], x_send, x_recv, partner)
    exchange.start()
    matmul(factor.at[child], right, series.at[now], block)
    exchange.wait_recv()

    for face in range(faces - 1):
        for distance in range(1, side):
            e_copies[face, distance].wait_recv()
        final_rows(rows_all.at[face], factor, out_ref, face * piece, 0, piece)
    for distance in range(1, side):
        e_copies[faces - 1, distance].wait_recv()

    for copy in [*s_copies.values(), *w_copies.values(), *e_copies.values(), *forwards, exchange]:
        copy.wait_send()


def local(child_maps, face_order):
    side = math.isqrt(lax.axis_size("tile"))
    count = side * side
    piece = child_maps.shape[2] // FACES
    order = side * piece
    dtype = child_maps.dtype
    faces = FACES - 1
    shared, window, exterior = extract(child_maps, face_order, piece)
    dma = pltpu.SemaphoreType.DMA
    held, rows_last, factor = pl.pallas_call(
        functools.partial(merge_kernel, side, piece),
        out_shape=[
            pltpu.VMEM(((faces - 1) * piece, 2 * CF * piece), dtype),
            pltpu.VMEM((side, piece, piece), dtype),
            pltpu.VMEM((2, order, CF * piece), dtype),
        ],
        in_specs=[pl.BlockSpec(memory_space=pl.ANY)] * 3,
        out_specs=[
            pl.BlockSpec(memory_space=pltpu.VMEM),
            pl.BlockSpec(memory_space=pltpu.VMEM),
            pl.BlockSpec(memory_space=pltpu.VMEM),
        ],
        scratch_shapes=[
            pltpu.VMEM((count, piece, piece), dtype),
            pltpu.VMEM((count, piece, piece), dtype),
            pltpu.VMEM((order, order), dtype),
            pltpu.VMEM((order, order), dtype),
            pltpu.VMEM((ITERS, order, order), dtype),
            pltpu.VMEM((side, piece, CF * piece), dtype),
            pltpu.VMEM((2, order, CF * piece), dtype),
            pltpu.VMEM((faces - 1, side, piece, piece), dtype),
            dma((count,)),
            dma((count,)),
            dma((side,)),
            dma((side,)),
            dma((faces, side)),
            dma((faces, side)),
            dma((count,)),
            dma((count,)),
            dma(()),
            dma(()),
            dma((2 + faces,)),
        ],
        compiler_params=pltpu.CompilerParams(
            collective_id=0, has_side_effects=True, vmem_limit_bytes=VMEM_LIMIT
        ),
        name="merge",
    )(shared, window, exterior)
    update = pl.pallas_call(
        functools.partial(finish_kernel, side, piece),
        out_shape=jax.ShapeDtypeStruct((faces * piece, 2 * CF * piece), dtype),
        in_specs=[
            pl.BlockSpec(memory_space=pl.ANY),
            pl.BlockSpec(memory_space=pltpu.VMEM),
            pl.BlockSpec(memory_space=pltpu.VMEM),
        ],
        out_specs=pl.BlockSpec(memory_space=pl.ANY),
        scratch_shapes=[
            pltpu.VMEM((piece, 2 * CF * piece), dtype),
            dma((FACES,)),
        ],
        compiler_params=pltpu.CompilerParams(vmem_limit_bytes=FINISH_LIMIT),
        name="finish",
    )(held, rows_last, factor)
    return update[None, None]


def solution(mesh):
    return jax.shard_map(
        local,
        mesh=mesh,
        in_specs=(P("pair", ("box", "tile"), None, None), P("box", None, None)),
        out_specs=P("pair", ("box", "tile"), None, None),
        check_vma=False,
    )
```
